256 devices in a mesh: gx: 32 (over z, x_lo, core), gy: 8 (over y, x_hi).
Axes of the slice: x: 4 (x_hi: 2, x_lo: 2; x = x_hi * 2 + x_lo), y: 4, z: 8, core: 2. Of those that a mesh axis runs over, the one named last changes fastest.
Arguments:
- density: float32 [256, 512, 256], P('gx', 'gy'), may hold values from 0 to 1
- sensitivity: float32 [256, 512, 256], P('gx', 'gy'), may hold values from -24 to 24
Outputs:
- projected: float32 [256, 512, 256], P('gx', 'gy')
- gradient: float32 [256, 512, 256], P('gx', 'gy')
The draws below stay inside these ranges and needn't reach their ends.
All inputs are finite; a program needn't handle non-finite values.
Results may differ from the reference program's by a relative error of at most 0.000021.
Values sent between devices are 32-bit elements; how exact they have to be, the bound alone decides.
No kernel may reach another device: no remote copies, remote signals or barrier semaphores. Data moves between devices by JAX's collectives and lax.ppermute only.
A program may use at most 64 MiB of HBM per device.

```python
import math
import jax
import jax.numpy as jnp

NZ = 256
RADIUS = 8
NX = 256
NY = 512


def draw_density(key, part):
    key = jax.random.fold_in(key, 11)
    key_phase, key_rough = jax.random.split(key, 2)
    phases = jax.random.uniform(key_phase, (3,), jnp.float32, 0.0, 2.0 * math.pi)
    xpos = jnp.arange(NX, dtype=jnp.float32)[:, None, None]
    ypos = jnp.arange(NY, dtype=jnp.float32)[None, :, None]
    zpos = jnp.arange(NZ, dtype=jnp.float32)[None, None, :]
    smooth = jnp.sin(2.0 * math.pi * 2.0 * xpos / NX + phases[0]) * jnp.cos(2.0 * math.pi * 3.0 * ypos / NY + phases[1])
    smooth = smooth * (0.7 + 0.3 * jnp.sin(2.0 * math.pi * zpos / NZ + phases[2]))
    rough = jax.random.uniform(key_rough, (NX, NY, NZ), jnp.float32, -1.0, 1.0)
    result = 0.5 + 0.25 * smooth + 0.2 * rough
    return result.astype(jnp.float32)


def steps_of(stream_key, shape, shards, smallest, high):
    loudness, own = 1.0, jax.random.fold_in(stream_key, 6)
    for dim, parts in shards:
        heights = jnp.exp(jax.random.uniform(jax.random.fold_in(own, dim), (parts,), jnp.float32, smallest / len(shards), high / len(shards)))
        loudness = loudness * jnp.repeat(heights, shape[dim] // parts).reshape([-1 if axis == dim else 1 for axis in range(len(shape))])
    return loudness


def bell_draw(own_key, shape, deviation, reach, pieces=(), held_as=jnp.bfloat16):
    array = jax.random.normal(own_key, shape, jnp.float32) * deviation
    if len(pieces) > 0:
        array = steps_of(own_key, shape, pieces, -0.22, 0.18) * array
    return jnp.clip(array, min=-reach, max=reach).astype(held_as)


def setup_inputs(seed: int = 0) -> dict:
    arg_keys = jax.random.split(jax.random.key(seed), 3)
    return {
        "density": draw_density(jax.random.fold_in(arg_keys[2], 71), 0),
        "sensitivity": bell_draw(arg_keys[1], (NX, NY, NZ), 4.0, 24.0, ((0, 32), (1, 8)), jnp.float32),
    }


sharpness = 8.0
threshold = 0.5


def cone_pass(field, axis):
    total = jnp.zeros_like(field)
    for offset in range(-RADIUS, RADIUS + 1):
        weight = (RADIUS + 1 - abs(offset)) / float((RADIUS + 1) ** 2)
        total = total + weight * jnp.roll(field, offset, axis)
    return total


def cone_filter(field):
    return cone_pass(cone_pass(cone_pass(field, 0), 1), 2)


def reference(density, sensitivity):
    filtered = cone_filter(density)
    tilted = jnp.tanh(sharpness * (filtered - threshold))
    scale_sum = jnp.tanh(sharpness * threshold) + jnp.tanh(sharpness * (1.0 - threshold))
    projected = (jnp.tanh(sharpness * threshold) + tilted) / scale_sum
    chain = sensitivity * (sharpness * (1.0 - tilted * tilted) / scale_sum)
    raw_gradient = cone_filter(chain)
    half_sym = 0.5 * (raw_gradient + raw_gradient[::-1, :, :])
    gradient = 0.5 * (half_sym + half_sym[:, ::-1, :])
    return projected, gradient
```

```python
import math

import jax
import jax.numpy as jnp
from jax import lax
from jax.experimental import pallas as pl
from jax.experimental.pallas import tpu as pltpu
from jax.sharding import PartitionSpec as P

RADIUS = 8
WIDTH = RADIUS + 1
SHARPNESS = 8.0
THRESHOLD = 0.5
TANH_LOW = math.tanh(SHARPNESS * THRESHOLD)
SCALE_SUM = TANH_LOW + math.tanh(SHARPNESS * (1.0 - THRESHOLD))
WEIGHT = 1.0 / float(WIDTH**6)
HALF = 64
F32 = jnp.float32


def run(body, outs, args, scratch=()):
    return pl.pallas_call(
        body,
        out_shape=[jax.ShapeDtypeStruct(shape, F32) for shape in outs],
        in_specs=[pl.BlockSpec(memory_space=pltpu.VMEM)] * len(args),
        out_specs=[pl.BlockSpec(memory_space=pltpu.VMEM)] * len(outs),
        scratch_shapes=list(scratch),
        compiler_params=pltpu.CompilerParams(vmem_limit_bytes=24 * 1024 * 1024),
    )(*args)


def box_list(items):
    pairs = [a + b for a, b in zip(items, items[1:])]
    fours = [a + b for a, b in zip(pairs, pairs[2:])]
    eights = [a + b for a, b in zip(fours, fours[4:])]
    return [a + b for a, b in zip(eights, items[8:])]


def cone_list(items):
    return box_list(box_list(items))


def ahead(field, step, axis):
    return pltpu.roll(field, field.shape[axis] - step, axis)


def box_rows(field, axis):
    pairs = field + ahead(field, 1, axis)
    fours = pairs + ahead(pairs, 2, axis)
    eights = fours + ahead(fours, 4, axis)
    return eights + ahead(field, 8, axis)


def cone_rows(field, axis):
    return box_rows(box_rows(field, axis), axis)


def reverse_eights(field, axis):
    size = field.shape[axis]
    row = lax.broadcasted_iota(jnp.int32, field.shape, axis)
    for bit in (1, 2, 4):
        field = jnp.where(
            (row & bit) == 0, pltpu.roll(field, size - bit, axis), pltpu.roll(field, bit, axis)
        )
    return field


def swap_halves(field):
    return pltpu.roll(field, HALF, field.ndim - 1)


def flip_planes(field):
    return jnp.stack([field[p] for p in reversed(range(field.shape[0]))])


def flip_rows(field):
    field = reverse_eights(field, 1)
    rows = field.shape[1]
    groups = [field[:, r : r + 8] for r in range(0, rows, 8)]
    return swap_halves(jnp.concatenate(groups[::-1], axis=1))


def first_lanes(shape):
    return lax.broadcasted_iota(jnp.int32, shape, len(shape) - 1) < HALF


def z_pass(field):
    count = field.shape[-1]
    row = lax.broadcasted_iota(jnp.int32, (count, count), 0)
    col = lax.broadcasted_iota(jnp.int32, (count, count), 1)
    gap = jnp.abs(row - col)
    taps = jnp.maximum(WIDTH - jnp.minimum(gap, count - gap), 0).astype(F32).astype(jnp.bfloat16)
    high = field.astype(jnp.bfloat16)
    rest = field - high.astype(F32)
    middle = rest.astype(jnp.bfloat16)
    low = (rest - middle.astype(F32)).astype(jnp.bfloat16)
    total = jnp.dot(low, taps, preferred_element_type=F32)
    total = total + jnp.dot(middle, taps, preferred_element_type=F32)
    return total + jnp.dot(high, taps, preferred_element_type=F32)


def solution(mesh):
    nx, ny = mesh.shape["gx"], mesh.shape["gy"]
    hx, hy = nx // 2, ny // 2

    def project_kernel(
        own, left, right, low, high, corner_l, corner_r, sens, projected, keep, to_x, to_y, to_xy, xs, ys
    ):
        planes, rows, depth = own.shape
        for lane in range(0, depth, 128):
            lanes = slice(lane, lane + 128)
            for group in range(rows // 8 + 2):
                if group == 0:
                    parts = ((corner_l, 0), (low, 0), (corner_r, 0))
                elif group == rows // 8 + 1:
                    parts = ((corner_l, 8), (high, 0), (corner_r, 8))
                else:
                    start = 8 * (group - 1)
                    parts = ((left, start), (own, start), (right, start))
                items = [ref[p, at : at + 8, lanes] for ref, at in parts for p in range(planes)]
                for p, item in enumerate(cone_list(items)):
                    xs[p, 8 * group : 8 * group + 8, lanes] = item
        for p in range(planes):
            ys[p * rows : (p + 1) * rows, :] = cone_rows(xs[p], 0)[:rows]
        filtered = z_pass(ys[...]) * WEIGHT
        tilted = jnp.tanh(SHARPNESS * (filtered - THRESHOLD))
        projected[...] = ((TANH_LOW + tilted) * (1.0 / SCALE_SUM)).reshape(planes, rows, depth)
        slope = (1.0 - tilted * tilted) * (SHARPNESS / SCALE_SUM)
        chain = sens[...] * slope.reshape(planes, rows, depth)
        upper_x = lax.axis_index("gx") >= hx
        upper_y = lax.axis_index("gy") >= hy
        near = jnp.where(upper_x, chain[:, :, 128:], chain[:, :, :128])
        far = jnp.where(upper_x, chain[:, :, :128], chain[:, :, 128:])
        for field, even_out, odd_out in ((near, keep, to_y), (far, to_x, to_xy)):
            top, bottom = field[:, : rows // 2], field[:, rows // 2 :]
            mask = first_lanes(top.shape)
            even = jnp.where(mask, top, swap_halves(bottom))
            odd = jnp.where(mask, swap_halves(top), bottom)
            even_out[...] = jnp.where(upper_y, odd, even)
            odd_out[...] = jnp.where(upper_y, even, odd)

    def sum_kernel(keep, from_x, from_y, from_xy, total, head, tail):
        other = flip_rows(from_y[...] + flip_planes(from_xy[...]))
        result = keep[...] + flip_planes(from_x[...]) + other
        total[...] = result
        head[...] = result[:, :8]
        tail[...] = result[:, -8:]

    def rows_kernel(field, from_low, from_high, out):
        own = field[...]
        rows = own.shape[1]
        head, tail = own[:, :8], own[:, -8:]
        mask = first_lanes(head.shape)
        place = lax.rem(lax.axis_index("gy"), hy)
        low = jnp.where(place == 0, reverse_eights(head, 1), swap_halves(from_low[...]))
        high = jnp.where(place == hy - 1, reverse_eights(tail, 1), swap_halves(from_high[...]))
        above = jnp.where(mask, low, swap_halves(tail))
        below = jnp.where(mask, swap_halves(head), high)
        padded = jnp.concatenate([above, own, below], axis=1)
        for p in range(own.shape[0]):
            out[p] = cone_rows(padded[p], 0)[:rows]

    def planes_kernel(own, left, right, out):
        planes, rows, _ = own.shape
        place = lax.rem(lax.axis_index("gx"), hx)
        first, last = place == 0, place == hx - 1
        for group in range(0, rows, 8):
            mine = [own[p, group : group + 8] for p in range(planes)]
            before = [jnp.where(first, mine[-1 - p], left[p, group : group + 8]) for p in range(planes)]
            after = [jnp.where(last, mine[-1 - p], right[p, group : group + 8]) for p in range(planes)]
            for p, item in enumerate(cone_list(before + mine + after)):
                out[p, group : group + 8] = item

    def finish_kernel(own, from_x, from_y, from_xy, gradient, flat):
        planes, rows, depth = gradient.shape
        upper_x = lax.axis_index("gx") >= hx
        upper_y = lax.axis_index("gy") >= hy
        near_own, near_y = own[...], flip_rows(from_y[...])
        far_x, far_xy = flip_planes(from_x[...]), flip_rows(flip_planes(from_xy[...]))
        sides = []
        for mine, other in ((near_own, near_y), (far_x, far_xy)):
            even, odd = jnp.where(upper_y, other, mine), jnp.where(upper_y, mine, other)
            mask = first_lanes(even.shape)
            top = jnp.where(mask, even, swap_halves(odd))
            bottom = jnp.where(mask, swap_halves(even), odd)
            sides.append(jnp.concatenate([top, bottom], axis=1).reshape(planes * rows, 128))
        near, far = sides
        flat[:, :128] = jnp.where(upper_x, far, near)
        flat[:, 128:] = jnp.where(upper_x, near, far)
        gradient[...] = (z_pass(flat[...]) * (0.25 * WEIGHT)).reshape(planes, rows, depth)

    both = [(i, j) for i in range(nx) for j in range(ny)]
    up_x = [(i, (i + 1) % nx) for i in range(nx)]
    down_x = [(b, a) for a, b in up_x]
    up_y = [(j, (j + 1) % ny) for j in range(ny)]
    down_y = [(b, a) for a, b in up_y]
    fold_up_x = [(a, b) for a, b in up_x if b % hx != 0]
    fold_down_x = [(b, a) for a, b in fold_up_x]
    fold_up_y = [(a, b) for a, b in up_y if b % hy != 0]
    fold_down_y = [(b, a) for a, b in fold_up_y]
    mirror_x = [(i, nx - 1 - i) for i in range(nx)]
    mirror_y = [(j, ny - 1 - j) for j in range(ny)]
    mirror_xy = [(i * ny + j, (nx - 1 - i) * ny + ny - 1 - j) for i, j in both]

    def mirrors(to_x, to_y, to_xy):
        return (
            lax.ppermute(to_x, "gx", mirror_x),
            lax.ppermute(to_y, "gy", mirror_y),
            lax.ppermute(to_xy, ("gx", "gy"), mirror_xy),
        )

    def local(density, sensitivity):
        block = density.shape
        planes, rows, depth = block
        packed = (planes, rows // 2, 128)
        edge = (planes, 8, 128)
        low = lax.ppermute(density[:, -8:], "gy", up_y)
        high = lax.ppermute(density[:, :8], "gy", down_y)
        left = lax.ppermute(density, "gx", up_x)
        right = lax.ppermute(density, "gx", down_x)
        edges = jnp.concatenate([low, high], axis=1)
        corner_l = lax.ppermute(edges, "gx", up_x)
        corner_r = lax.ppermute(edges, "gx", down_x)
        projected, keep, to_x, to_y, to_xy = run(
            project_kernel,
            [block, packed, packed, packed, packed],
            (density, left, right, low, high, corner_l, corner_r, sensitivity),
            (pltpu.VMEM((planes, rows + 16, depth), F32), pltpu.VMEM((planes * rows, depth), F32)),
        )
        total, head, tail = run(sum_kernel, [packed, edge, edge], (keep, *mirrors(to_x, to_y, to_xy)))
        from_low = lax.ppermute(tail, "gy", fold_up_y)
        from_high = lax.ppermute(head, "gy", fold_down_y)
        (smooth,) = run(rows_kernel, [packed], (total, from_low, from_high))
        before = lax.ppermute(smooth, "gx", fold_up_x)
        after = lax.ppermute(smooth, "gx", fold_down_x)
        (quarter,) = run(planes_kernel, [packed], (smooth, before, after))
        (gradient,) = run(
            finish_kernel,
            [block],
            (quarter, *mirrors(quarter, quarter, quarter)),
            (pltpu.VMEM((planes * rows, depth), F32),),
        )
        return projected, gradient

    return jax.shard_map(
        local,
        mesh=mesh,
        in_specs=(P("gx", "gy", None), P("gx", "gy", None)),
        out_specs=(P("gx", "gy", None), P("gx", "gy", None)),
        check_vma=False,
    )
```

```python
import math

import jax
import jax.numpy as jnp
from jax import lax
from jax.experimental import pallas as pl
from jax.experimental.pallas import tpu as pltpu
from jax.sharding import PartitionSpec as P

RADIUS = 8
WIDTH = RADIUS + 1
EDGE = 2 * RADIUS
SHARPNESS = 8.0
THRESHOLD = 0.5
TANH_LOW = math.tanh(SHARPNESS * THRESHOLD)
SCALE_SUM = TANH_LOW + math.tanh(SHARPNESS * (1.0 - THRESHOLD))
WEIGHT = 1.0 / float(WIDTH**6)
HALF = 64
F32 = jnp.float32


def run(body, outs, args, scratch=()):
    return pl.pallas_call(
        body,
        out_shape=[jax.ShapeDtypeStruct(shape, F32) for shape in outs],
        in_specs=[pl.BlockSpec(memory_space=pltpu.VMEM)] * len(args),
        out_specs=[pl.BlockSpec(memory_space=pltpu.VMEM)] * len(outs),
        scratch_shapes=list(scratch),
        compiler_params=pltpu.CompilerParams(vmem_limit_bytes=24 * 1024 * 1024),
    )(*args)


def box_list(items):
    pairs = [a + b for a, b in zip(items, items[1:])]
    fours = [a + b for a, b in zip(pairs, pairs[2:])]
    eights = [a + b for a, b in zip(fours, fours[4:])]
    return [a + b for a, b in zip(eights, items[8:])]


def cone_list(items):
    return box_list(box_list(items))


def ahead(field, step, axis):
    return pltpu.roll(field, field.shape[axis] - step, axis)


def box_rows(field, axis):
    pairs = field + ahead(field, 1, axis)
    fours = pairs + ahead(pairs, 2, axis)
    eights = fours + ahead(fours, 4, axis)
    return eights + ahead(field, 8, axis)


def cone_rows(field, axis):
    return box_rows(box_rows(field, axis), axis)


def reverse_eights(field, axis):
    size = field.shape[axis]
    row = lax.broadcasted_iota(jnp.int32, field.shape, axis)
    for bit in (1, 2, 4):
        field = jnp.where(
            (row & bit) == 0, pltpu.roll(field, size - bit, axis), pltpu.roll(field, bit, axis)
        )
    return field


def swap_halves(field):
    return pltpu.roll(field, HALF, field.ndim - 1)


def flip_planes(field):
    return jnp.stack([field[p] for p in reversed(range(field.shape[0]))])


def flip_rows(field):
    field = reverse_eights(field, 1)
    rows = field.shape[1]
    groups = [field[:, r : r + 8] for r in range(0, rows, 8)]
    return swap_halves(jnp.concatenate(groups[::-1], axis=1))


def first_lanes(shape):
    return lax.broadcasted_iota(jnp.int32, shape, len(shape) - 1) < HALF


def z_pass(field, pieces):
    count = field.shape[-1]
    row = lax.broadcasted_iota(jnp.int32, (count, count), 0)
    col = lax.broadcasted_iota(jnp.int32, (count, count), 1)
    gap = jnp.abs(row - col)
    taps = jnp.maximum(WIDTH - jnp.minimum(gap, count - gap), 0).astype(F32).astype(jnp.bfloat16)
    total = None
    for _ in range(pieces):
        piece = field.astype(jnp.bfloat16)
        field = field - piece.astype(F32)
        part = jnp.dot(piece, taps, preferred_element_type=F32)
        total = part if total is None else total + part
    return total


def solution(mesh):
    nx, ny = mesh.shape["gx"], mesh.shape["gy"]
    hx, hy = nx // 2, ny // 2

    def ordered(odd, near, far):
        return jnp.where(odd, near, far), jnp.where(odd, far, near)

    def is_odd(axis):
        return lax.rem(lax.axis_index(axis), 2) == 1

    def across(own, near, far, odd, row, lanes, first=None, last=None):
        planes = own.shape[0]
        rows = slice(row, row + 8)
        mine = [own[p, rows, lanes] for p in range(planes)]
        before, after = [], []
        for p in range(planes):
            b, a = ordered(odd, near[p, rows, lanes], far[p, rows, lanes])
            before.append(b if first is None else jnp.where(first, mine[-1 - p], b))
            after.append(a if last is None else jnp.where(last, mine[-1 - p], a))
        return cone_list(before + mine + after)

    def hold_kernel(first, second, first_out, second_out):
        first_out[...] = first[...]
        second_out[...] = second[...]

    def cross_edges_kernel(own, near, far, sens, to_near, to_far):
        planes, rows, depth = own.shape
        odd_x, odd_y = is_odd("gx"), is_odd("gy")
        for lane in range(0, depth, 128):
            lanes = slice(lane, lane + 128)
            for row in range(0, EDGE, 8):
                heads = across(own, near, far, odd_x, row, lanes)
                tails = across(own, near, far, odd_x, rows - EDGE + row, lanes)
                for p, (head, tail) in enumerate(zip(heads, tails)):
                    to_near[p, row : row + 8, lanes] = jnp.where(odd_y, head, tail)
                    to_far[p, row : row + 8, lanes] = jnp.where(odd_y, tail, head)
        head, tail = sens[:, :RADIUS], sens[:, rows - RADIUS :]
        to_near[:, EDGE:] = jnp.where(odd_y, head, tail)
        to_far[:, EDGE:] = jnp.where(odd_y, tail, head)

    def cross_body_kernel(own, near, far, edge_near, edge_far, out, flat):
        planes, rows, depth = own.shape
        odd_x = is_odd("gx")
        head, tail = ordered(is_odd("gy"), edge_near[:, :EDGE], edge_far[:, :EDGE])
        for p in range(planes):
            flat[p * rows : p * rows + EDGE, :] = head[p]
            flat[(p + 1) * rows - EDGE : (p + 1) * rows, :] = tail[p]
        for lane in range(0, depth, 128):
            lanes = slice(lane, lane + 128)
            for row in range(EDGE, rows - EDGE, 8):
                for p, item in enumerate(across(own, near, far, odd_x, row, lanes)):
                    flat[p * rows + row : p * rows + row + 8, lanes] = item
        out[...] = z_pass(flat[...], 3).reshape(planes, rows, depth)

    def chain_kernel(own, near, far, sens, tilted_out, keep, to_x, to_y, to_xy, halo, ys):
        planes, rows, depth = own.shape
        wide = rows + 2 * RADIUS
        low, high = ordered(is_odd("gy"), near[...], far[...])
        for p in range(planes):
            halo[2 * EDGE * p : 2 * EDGE * p + EDGE, :] = low[p, :EDGE]
            halo[2 * EDGE * p + EDGE : 2 * EDGE * (p + 1), :] = high[p, :EDGE]
        outer = z_pass(halo[...], 3).reshape(planes, 2 * EDGE, depth)
        for p in range(planes):
            padded = jnp.concatenate([outer[p, :EDGE], own[p], outer[p, EDGE:]], axis=0)
            ys[p] = cone_rows(padded, 0)[:wide]
        filtered = ys[...] * WEIGHT
        tilted = jnp.tanh(SHARPNESS * (filtered - THRESHOLD))
        tilted_out[...] = tilted[:, RADIUS : RADIUS + rows]
        slope = (1.0 - tilted * tilted) * (SHARPNESS / SCALE_SUM)
        chain = jnp.concatenate([low[:, EDGE:], sens[...], high[:, EDGE:]], axis=1) * slope
        upper_x = lax.axis_index("gx") >= hx
        upper_y = lax.axis_index("gy") >= hy
        near = jnp.where(upper_x, chain[:, :, 128:], chain[:, :, :128])
        far = jnp.where(upper_x, chain[:, :, :128], chain[:, :, 128:])
        for field, even_out, odd_out in ((near, keep, to_y), (far, to_x, to_xy)):
            top, bottom = field[:, : wide // 2], field[:, wide // 2 :]
            mask = first_lanes(top.shape)
            even = jnp.where(mask, top, swap_halves(bottom))
            odd = jnp.where(mask, swap_halves(top), bottom)
            even_out[...] = jnp.where(upper_y, odd, even)
            odd_out[...] = jnp.where(upper_y, even, odd)

    def project_kernel(tilted, projected):
        projected[...] = (TANH_LOW + tilted[...]) * (1.0 / SCALE_SUM)

    def sum_kernel(keep, from_x, from_y, from_xy, out):
        other = flip_rows(from_y[...] + flip_planes(from_xy[...]))
        total = keep[...] + flip_planes(from_x[...]) + other
        rows = total.shape[1]
        swapped = swap_halves(total)
        upper = jnp.concatenate([total, swapped[:, :8]], axis=1)
        lower = jnp.concatenate([swapped[:, rows - 8 :], total], axis=1)
        padded = jnp.where(first_lanes(upper.shape), upper, lower)
        for p in range(total.shape[0]):
            out[p] = cone_rows(padded[p], 0)[: out.shape[1]]

    def cross_quarter_kernel(own, near, far, out):
        planes, rows, depth = own.shape
        place = lax.rem(lax.axis_index("gx"), hx)
        first, last = place == 0, place == hx - 1
        for row in range(0, rows, 8):
            items = across(own, near, far, is_odd("gx"), row, slice(0, depth), first, last)
            for p, item in enumerate(items):
                out[p, row : row + 8, :] = item

    def finish_kernel(own, from_x, from_y, from_xy, gradient, flat):
        planes, rows, depth = gradient.shape
        upper_x = lax.axis_index("gx") >= hx
        upper_y = lax.axis_index("gy") >= hy
        near_own, near_y = own[...], flip_rows(from_y[...])
        far_x, far_xy = flip_planes(from_x[...]), flip_rows(flip_planes(from_xy[...]))
        sides = []
        for mine, other in ((near_own, near_y), (far_x, far_xy)):
            even, odd = jnp.where(upper_y, other, mine), jnp.where(upper_y, mine, other)
            mask = first_lanes(even.shape)
            top = jnp.where(mask, even, swap_halves(odd))
            bottom = jnp.where(mask, swap_halves(even), odd)
            sides.append(jnp.concatenate([top, bottom], axis=1).reshape(planes * rows, 128))
        near, far = sides
        flat[:, :128] = jnp.where(upper_x, far, near)
        flat[:, 128:] = jnp.where(upper_x, near, far)
        gradient[...] = (z_pass(flat[...], 2) * (0.25 * WEIGHT)).reshape(planes, rows, depth)

    both = [(i, j) for i in range(nx) for j in range(ny)]
    near_x = [(i, i ^ 1) for i in range(nx)]
    near_y = [(j, j ^ 1) for j in range(ny)]
    far_x = [(i, (i + (1 if i % 2 else -1)) % nx) for i in range(nx)]
    far_y = [(j, (j + (1 if j % 2 else -1)) % ny) for j in range(ny)]
    fold_far_x = [(a, b) for a, b in far_x if a // hx == b // hx and abs(a - b) == 1]
    mirror_x = [(i, nx - 1 - i) for i in range(nx)]
    mirror_y = [(j, ny - 1 - j) for j in range(ny)]
    mirror_xy = [(i * ny + j, (nx - 1 - i) * ny + ny - 1 - j) for i, j in both]

    def mirrors(to_x, to_y, to_xy):
        from_xy = lax.ppermute(to_xy, ("gx", "gy"), mirror_xy)
        from_y = lax.ppermute(to_y, "gy", mirror_y)
        from_x = lax.ppermute(to_x, "gx", mirror_x)
        return from_x, from_y, from_xy

    def local(density, sensitivity):
        block = density.shape
        planes, rows, depth = block
        packed = (planes, rows // 2, 128)
        wide = (planes, rows // 2 + RADIUS, 128)
        flat = pltpu.VMEM((planes * rows, depth), F32)
        far = lax.ppermute(density, "gx", far_x)
        near = lax.ppermute(density, "gx", near_x)
        own, sens = run(hold_kernel, [block, block], (density, sensitivity))
        to_near, to_far = run(
            cross_edges_kernel, [(planes, EDGE + RADIUS, depth)] * 2, (own, near, far, sens)
        )
        from_far = lax.ppermute(to_far, "gy", far_y)
        from_near = lax.ppermute(to_near, "gy", near_y)
        (crossed,) = run(cross_body_kernel, [block], (own, near, far, to_near, to_far), (flat,))
        tilted, keep, to_x, to_y, to_xy = run(
            chain_kernel,
            [block, wide, wide, wide, wide],
            (crossed, from_near, from_far, sens),
            (
                pltpu.VMEM((planes * 2 * EDGE, depth), F32),
                pltpu.VMEM((planes, rows + 2 * RADIUS, depth), F32),
            ),
        )
        from_mirrors = mirrors(to_x, to_y, to_xy)
        (projected,) = run(project_kernel, [block], (tilted,))
        (smooth,) = run(sum_kernel, [packed], (keep, *from_mirrors))
        far = lax.ppermute(smooth, "gx", fold_far_x)
        near = lax.ppermute(smooth, "gx", near_x)
        (quarter,) = run(cross_quarter_kernel, [packed], (smooth, near, far))
        (gradient,) = run(
            finish_kernel,
            [block],
            (quarter, *mirrors(quarter, quarter, quarter)),
            (flat,),
        )
        return projected, gradient

    return jax.shard_map(
        local,
        mesh=mesh,
        in_specs=(P("gx", "gy", None), P("gx", "gy", None)),
        out_specs=(P("gx", "gy", None), P("gx", "gy", None)),
        check_vma=False,
    )
```

```python
import math

import jax
import jax.numpy as jnp
from jax import lax
from jax.experimental import pallas as pl
from jax.experimental.pallas import tpu as pltpu
from jax.sharding import PartitionSpec as P

RADIUS = 8
WIDTH = RADIUS + 1
EDGE = 2 * RADIUS
SHARPNESS = 8.0
THRESHOLD = 0.5
TANH_LOW = math.tanh(SHARPNESS * THRESHOLD)
SCALE_SUM = TANH_LOW + math.tanh(SHARPNESS * (1.0 - THRESHOLD))
WEIGHT = 1.0 / float(WIDTH**6)
HALF = 64
F32 = jnp.float32


def run(body, outs, args, scratch=()):
    return pl.pallas_call(
        body,
        out_shape=[jax.ShapeDtypeStruct(shape, F32) for shape in outs],
        in_specs=[pl.BlockSpec(memory_space=pltpu.VMEM)] * len(args),
        out_specs=[pl.BlockSpec(memory_space=pltpu.VMEM)] * len(outs),
        scratch_shapes=list(scratch),
        compiler_params=pltpu.CompilerParams(vmem_limit_bytes=24 * 1024 * 1024),
    )(*args)


def box_list(items):
    pairs = [a + b for a, b in zip(items, items[1:])]
    fours = [a + b for a, b in zip(pairs, pairs[2:])]
    eights = [a + b for a, b in zip(fours, fours[4:])]
    return [a + b for a, b in zip(eights, items[8:])]


def cone_list(items):
    return box_list(box_list(items))


def ahead(field, step, axis):
    return pltpu.roll(field, field.shape[axis] - step, axis)


def box_rows(field, axis):
    pairs = field + ahead(field, 1, axis)
    fours = pairs + ahead(pairs, 2, axis)
    eights = fours + ahead(fours, 4, axis)
    return eights + ahead(field, 8, axis)


def cone_rows(field, axis):
    return box_rows(box_rows(field, axis), axis)


def reverse_eights(field, axis):
    size = field.shape[axis]
    row = lax.broadcasted_iota(jnp.int32, field.shape, axis)
    for bit in (1, 2, 4):
        field = jnp.where(
            (row & bit) == 0, pltpu.roll(field, size - bit, axis), pltpu.roll(field, bit, axis)
        )
    return field


def swap_halves(field):
    return pltpu.roll(field, HALF, field.ndim - 1)


def flip_planes(field):
    return jnp.stack([field[p] for p in reversed(range(field.shape[0]))])


def flip_rows(field):
    field = reverse_eights(field, 1)
    rows = field.shape[1]
    groups = [field[:, r : r + 8] for r in range(0, rows, 8)]
    return swap_halves(jnp.concatenate(groups[::-1], axis=1))


def first_lanes(shape):
    return lax.broadcasted_iota(jnp.int32, shape, len(shape) - 1) < HALF


def z_pass(field, pieces):
    count = field.shape[-1]
    row = lax.broadcasted_iota(jnp.int32, (count, count), 0)
    col = lax.broadcasted_iota(jnp.int32, (count, count), 1)
    gap = jnp.abs(row - col)
    taps = jnp.maximum(WIDTH - jnp.minimum(gap, count - gap), 0).astype(F32).astype(jnp.bfloat16)
    total = None
    for _ in range(pieces):
        piece = field.astype(jnp.bfloat16)
        field = field - piece.astype(F32)
        part = jnp.dot(piece, taps, preferred_element_type=F32)
        total = part if total is None else total + part
    return total


def solution(mesh):
    nx, ny = mesh.shape["gx"], mesh.shape["gy"]
    hx, hy = nx // 2, ny // 2

    def ordered(odd, near, far):
        return jnp.where(odd, near, far), jnp.where(odd, far, near)

    def is_odd(axis):
        return lax.rem(lax.axis_index(axis), 2) == 1

    def across(own, near, far, odd, row, lanes, first=None, last=None):
        planes = own.shape[0]
        rows = slice(row, row + 8)
        mine = [own[p, rows, lanes] for p in range(planes)]
        before, after = [], []
        for p in range(planes):
            b, a = ordered(odd, near[p, rows, lanes], far[p, rows, lanes])
            before.append(b if first is None else jnp.where(first, mine[-1 - p], b))
            after.append(a if last is None else jnp.where(last, mine[-1 - p], a))
        return cone_list(before + mine + after)

    def tilt(total):
        tilted = jnp.tanh(SHARPNESS * (total * WEIGHT - THRESHOLD))
        return tilted, (1.0 - tilted * tilted) * (SHARPNESS / SCALE_SUM)

    def hold_kernel(first, second, first_out, second_out):
        first_out[...] = first[...]
        second_out[...] = second[...]

    def cross_edges_kernel(own, near, far, sens, to_near, to_far):
        planes, rows, depth = own.shape
        odd_x, odd_y = is_odd("gx"), is_odd("gy")
        for lane in range(0, depth, 128):
            lanes = slice(lane, lane + 128)
            for row in range(0, EDGE, 8):
                heads = across(own, near, far, odd_x, row, lanes)
                tails = across(own, near, far, odd_x, rows - EDGE + row, lanes)
                for p, (head, tail) in enumerate(zip(heads, tails)):
                    to_near[p, row : row + 8, lanes] = jnp.where(odd_y, head, tail)
                    to_far[p, row : row + 8, lanes] = jnp.where(odd_y, tail, head)
        head, tail = sens[:, :RADIUS], sens[:, rows - RADIUS :]
        to_near[:, EDGE:] = jnp.where(odd_y, head, tail)
        to_far[:, EDGE:] = jnp.where(odd_y, tail, head)

    def cross_body_kernel(own, near, far, edge_near, edge_far, sens, outer, tilted_out, chain, middle, flat):
        planes, rows, depth = own.shape
        odd_x = is_odd("gx")
        head, tail = ordered(is_odd("gy"), edge_near[:, :EDGE], edge_far[:, :EDGE])
        for p in range(planes):
            flat[p * rows : p * rows + EDGE, :] = head[p]
            flat[(p + 1) * rows - EDGE : (p + 1) * rows, :] = tail[p]
        for lane in range(0, depth, 128):
            lanes = slice(lane, lane + 128)
            for row in range(EDGE, rows - EDGE, 8):
                for p, item in enumerate(across(own, near, far, odd_x, row, lanes)):
                    flat[p * rows + row : p * rows + row + 8, lanes] = item
        crossed = z_pass(flat[...], 3).reshape(planes, rows, depth)
        outer[:, :EDGE] = crossed[:, :EDGE]
        outer[:, EDGE:] = crossed[:, rows - EDGE :]
        inside = rows - 2 * RADIUS
        for p in range(planes):
            tilted, slope = tilt(cone_rows(crossed[p], 0)[:inside])
            tilted_out[p] = tilted
            part = sens[p, RADIUS : rows - RADIUS] * slope
            chain[p] = part
            middle[p] = cone_rows(part, 0)[: rows - 2 * EDGE]

    def chain_kernel(
        outer, chain_in, middle, near, far, sens, tilted_out, keep, to_x, to_y, to_xy, halo, ys
    ):
        planes, rows, depth = sens.shape
        low, high = ordered(is_odd("gy"), near[...], far[...])
        for p in range(planes):
            halo[2 * EDGE * p : 2 * EDGE * p + EDGE, :] = low[p, :EDGE]
            halo[2 * EDGE * p + EDGE : 2 * EDGE * (p + 1), :] = high[p, :EDGE]
        beyond = z_pass(halo[...], 3).reshape(planes, 2 * EDGE, depth)
        for p in range(planes):
            top = jnp.concatenate([beyond[p, :EDGE], outer[p, :EDGE]], axis=0)
            bottom = jnp.concatenate([outer[p, EDGE:], beyond[p, EDGE:]], axis=0)
            tops, slope_top = tilt(cone_rows(top, 0)[:EDGE])
            bottoms, slope_bottom = tilt(cone_rows(bottom, 0)[:EDGE])
            tilted_out[p, :RADIUS] = tops[RADIUS:]
            tilted_out[p, RADIUS:] = bottoms[:RADIUS]
            above = jnp.concatenate([low[p, EDGE:], sens[p, :RADIUS]], axis=0) * slope_top
            below = jnp.concatenate([sens[p, rows - RADIUS :], high[p, EDGE:]], axis=0) * slope_bottom
            top = jnp.concatenate([above, chain_in[p, :EDGE]], axis=0)
            bottom = jnp.concatenate([chain_in[p, rows - EDGE - 2 * RADIUS :], below], axis=0)
            ys[p, :EDGE] = cone_rows(top, 0)[:EDGE]
            ys[p, EDGE : rows - EDGE] = middle[p]
            ys[p, rows - EDGE :] = cone_rows(bottom, 0)[:EDGE]
        chain = ys[...]
        upper_x = lax.axis_index("gx") >= hx
        upper_y = lax.axis_index("gy") >= hy
        near = jnp.where(upper_x, chain[:, :, 128:], chain[:, :, :128])
        far = jnp.where(upper_x, chain[:, :, :128], chain[:, :, 128:])
        for field, even_out, odd_out in ((near, keep, to_y), (far, to_x, to_xy)):
            top, bottom = field[:, : rows // 2], field[:, rows // 2 :]
            mask = first_lanes(top.shape)
            even = jnp.where(mask, top, swap_halves(bottom))
            odd = jnp.where(mask, swap_halves(top), bottom)
            even_out[...] = jnp.where(upper_y, odd, even)
            odd_out[...] = jnp.where(upper_y, even, odd)

    def project_kernel(inside, edges, projected):
        tilted = jnp.concatenate([edges[:, :RADIUS], inside[...], edges[:, RADIUS:]], axis=1)
        projected[...] = (TANH_LOW + tilted) * (1.0 / SCALE_SUM)

    def sum_kernel(keep, from_x, from_xy, from_y, total):
        other = flip_rows(from_y[...] + flip_planes(from_xy[...]))
        total[...] = keep[...] + flip_planes(from_x[...]) + other

    def cross_quarter_kernel(own, near, far, out):
        planes, rows, depth = own.shape
        place = lax.rem(lax.axis_index("gx"), hx)
        first, last = place == 0, place == hx - 1
        for row in range(0, rows, 8):
            items = across(own, near, far, is_odd("gx"), row, slice(0, depth), first, last)
            for p, item in enumerate(items):
                out[p, row : row + 8, :] = item

    def finish_kernel(own, from_y, from_xy, from_x, gradient, flat):
        planes, rows, depth = gradient.shape
        upper_x = lax.axis_index("gx") >= hx
        upper_y = lax.axis_index("gy") >= hy
        near_own, near_y = own[...], flip_rows(from_y[...])
        far_x, far_xy = flip_planes(from_x[...]), flip_rows(flip_planes(from_xy[...]))
        sides = []
        for mine, other in ((near_own, near_y), (far_x, far_xy)):
            even, odd = jnp.where(upper_y, other, mine), jnp.where(upper_y, mine, other)
            mask = first_lanes(even.shape)
            top = jnp.where(mask, even, swap_halves(odd))
            bottom = jnp.where(mask, swap_halves(even), odd)
            sides.append(jnp.concatenate([top, bottom], axis=1).reshape(planes * rows, 128))
        near, far = sides
        flat[:, :128] = jnp.where(upper_x, far, near)
        flat[:, 128:] = jnp.where(upper_x, near, far)
        gradient[...] = (z_pass(flat[...], 2) * (0.25 * WEIGHT)).reshape(planes, rows, depth)

    both = [(i, j) for i in range(nx) for j in range(ny)]
    near_x = [(i, i ^ 1) for i in range(nx)]
    near_y = [(j, j ^ 1) for j in range(ny)]
    far_x = [(i, (i + (1 if i % 2 else -1)) % nx) for i in range(nx)]
    far_y = [(j, (j + (1 if j % 2 else -1)) % ny) for j in range(ny)]
    fold_far_x = [(a, b) for a, b in far_x if a // hx == b // hx and abs(a - b) == 1]
    mirror_x = [(i, nx - 1 - i) for i in range(nx)]
    mirror_y = [(j, ny - 1 - j) for j in range(ny)]
    mirror_xy = [(i * ny + j, (nx - 1 - i) * ny + ny - 1 - j) for i, j in both]

    def mirrors(to_x, to_y, to_xy):
        from_x = lax.ppermute(to_x, "gx", mirror_x)
        from_xy = lax.ppermute(to_xy, ("gx", "gy"), mirror_xy)
        from_y = lax.ppermute(to_y, "gy", mirror_y)
        return from_x, from_y, from_xy

    def local(density, sensitivity):
        block = density.shape
        planes, rows, depth = block
        packed = (planes, rows // 2, 128)
        flat = pltpu.VMEM((planes * rows, depth), F32)
        far = lax.ppermute(density, "gx", far_x)
        near = lax.ppermute(density, "gx", near_x)
        own, sens = run(hold_kernel, [block, block], (density, sensitivity))
        to_near, to_far = run(
            cross_edges_kernel, [(planes, EDGE + RADIUS, depth)] * 2, (own, near, far, sens)
        )
        from_far = lax.ppermute(to_far, "gy", far_y)
        from_near = lax.ppermute(to_near, "gy", near_y)
        outer, inside, chain, middle = run(
            cross_body_kernel,
            [
                (planes, 2 * EDGE, depth),
                (planes, rows - 2 * RADIUS, depth),
                (planes, rows - 2 * RADIUS, depth),
                (planes, rows - 2 * EDGE, depth),
            ],
            (own, near, far, to_near, to_far, sens),
            (flat,),
        )
        edges, keep, to_x, to_y, to_xy = run(
            chain_kernel,
            [(planes, 2 * RADIUS, depth), packed, packed, packed, packed],
            (outer, chain, middle, from_near, from_far, sens),
            (pltpu.VMEM((planes * 2 * EDGE, depth), F32), pltpu.VMEM(block, F32)),
        )
        from_x, from_y, from_xy = mirrors(to_x, to_y, to_xy)
        (projected,) = run(project_kernel, [block], (inside, edges))
        (total,) = run(sum_kernel, [packed], (keep, from_x, from_xy, from_y))
        far = lax.ppermute(total, "gx", fold_far_x)
        near = lax.ppermute(total, "gx", near_x)
        (quarter,) = run(cross_quarter_kernel, [packed], (total, near, far))
        from_x, from_y, from_xy = mirrors(quarter, quarter, quarter)
        (gradient,) = run(
            finish_kernel,
            [block],
            (quarter, from_y, from_xy, from_x),
            (flat,),
        )
        return projected, gradient

    return jax.shard_map(
        local,
        mesh=mesh,
        in_specs=(P("gx", "gy", None), P("gx", "gy", None)),
        out_specs=(P("gx", "gy", None), P("gx", "gy", None)),
        check_vma=False,
    )
```

```python
import math

import jax
import jax.numpy as jnp
from jax import lax
from jax.experimental import pallas as pl
from jax.experimental.pallas import tpu as pltpu
from jax.sharding import PartitionSpec as P

RADIUS = 8
WIDTH = RADIUS + 1
EDGE = 2 * RADIUS
SHARPNESS = 8.0
THRESHOLD = 0.5
TANH_LOW = math.tanh(SHARPNESS * THRESHOLD)
SCALE_SUM = TANH_LOW + math.tanh(SHARPNESS * (1.0 - THRESHOLD))
WEIGHT = 1.0 / float(WIDTH**6)
F32 = jnp.float32


def run(body, outs, args, scratch=()):
    return pl.pallas_call(
        body,
        out_shape=[jax.ShapeDtypeStruct(shape, F32) for shape in outs],
        in_specs=[pl.BlockSpec(memory_space=pltpu.VMEM)] * len(args),
        out_specs=[pl.BlockSpec(memory_space=pltpu.VMEM)] * len(outs),
        scratch_shapes=list(scratch),
        compiler_params=pltpu.CompilerParams(vmem_limit_bytes=24 * 1024 * 1024),
    )(*args)


def box_list(items):
    pairs = [a + b for a, b in zip(items, items[1:])]
    fours = [a + b for a, b in zip(pairs, pairs[2:])]
    eights = [a + b for a, b in zip(fours, fours[4:])]
    return [a + b for a, b in zip(eights, items[8:])]


def cone_list(items):
    return box_list(box_list(items))


def ahead(field, step, axis):
    return pltpu.roll(field, field.shape[axis] - step, axis)


def box_rows(field, axis):
    pairs = field + ahead(field, 1, axis)
    fours = pairs + ahead(pairs, 2, axis)
    eights = fours + ahead(fours, 4, axis)
    return eights + ahead(field, 8, axis)


def cone_rows(field, axis):
    return box_rows(box_rows(field, axis), axis)


def reverse_eights(field, axis):
    size = field.shape[axis]
    row = lax.broadcasted_iota(jnp.int32, field.shape, axis)
    for bit in (1, 2, 4):
        field = jnp.where(
            (row & bit) == 0, pltpu.roll(field, size - bit, axis), pltpu.roll(field, bit, axis)
        )
    return field


def flip_planes(field):
    return jnp.stack([field[p] for p in reversed(range(field.shape[0]))])


def flip_rows(field):
    field = reverse_eights(field, 1)
    groups = [field[:, r : r + 8] for r in range(0, field.shape[1], 8)]
    return jnp.concatenate(groups[::-1], axis=1)


def z_pass(field, pieces):
    count = field.shape[-1]
    row = lax.broadcasted_iota(jnp.int32, (count, count), 0)
    col = lax.broadcasted_iota(jnp.int32, (count, count), 1)
    gap = jnp.abs(row - col)
    taps = jnp.maximum(WIDTH - jnp.minimum(gap, count - gap), 0).astype(F32).astype(jnp.bfloat16)
    total = None
    for _ in range(pieces):
        piece = field.astype(jnp.bfloat16)
        field = field - piece.astype(F32)
        part = jnp.dot(piece, taps, preferred_element_type=F32)
        total = part if total is None else total + part
    return total


def solution(mesh):
    nx, ny = mesh.shape["gx"], mesh.shape["gy"]
    hx, hy = nx // 2, ny // 2

    def ordered(odd, near, far):
        return jnp.where(odd, near, far), jnp.where(odd, far, near)

    def is_odd(axis):
        return lax.rem(lax.axis_index(axis), 2) == 1

    def across(own, near, far, odd, row, lanes, first=None, last=None):
        planes = own.shape[0]
        rows = slice(row, row + 8)
        mine = [own[p, rows, lanes] for p in range(planes)]
        before, after = [], []
        for p in range(planes):
            b, a = ordered(odd, near[p, rows, lanes], far[p, rows, lanes])
            before.append(b if first is None else jnp.where(first, mine[-1 - p], b))
            after.append(a if last is None else jnp.where(last, mine[-1 - p], a))
        return cone_list(before + mine + after)

    def tilt(total):
        tilted = jnp.tanh(SHARPNESS * (total * WEIGHT - THRESHOLD))
        return tilted, (1.0 - tilted * tilted) * (SHARPNESS / SCALE_SUM)

    def halves(field):
        half = field.shape[-1] // 2
        upper = lax.axis_index("gy") >= hy
        low, high = field[..., :half], field[..., half:]
        return jnp.where(upper, high, low), jnp.where(upper, low, high)

    def hold_kernel(first, second, first_out, second_out):
        first_out[...] = first[...]
        second_out[...] = second[...]

    def cross_edges_kernel(own, near, far, sens, to_near, to_far):
        planes, rows, depth = own.shape
        odd_x, odd_y = is_odd("gx"), is_odd("gy")
        for lane in range(0, depth, 128):
            lanes = slice(lane, lane + 128)
            for row in range(0, EDGE, 8):
                heads = across(own, near, far, odd_x, row, lanes)
                tails = across(own, near, far, odd_x, rows - EDGE + row, lanes)
                for p, (head, tail) in enumerate(zip(heads, tails)):
                    to_near[p, row : row + 8, lanes] = jnp.where(odd_y, head, tail)
                    to_far[p, row : row + 8, lanes] = jnp.where(odd_y, tail, head)
        head, tail = sens[:, :RADIUS], sens[:, rows - RADIUS :]
        to_near[:, EDGE:] = jnp.where(odd_y, head, tail)
        to_far[:, EDGE:] = jnp.where(odd_y, tail, head)

    def cross_body_kernel(own, near, far, edge_near, edge_far, sens, outer, tilted_out, chain, keep, send, flat, middle):
        planes, rows, depth = own.shape
        odd_x = is_odd("gx")
        head, tail = ordered(is_odd("gy"), edge_near[:, :EDGE], edge_far[:, :EDGE])
        for p in range(planes):
            flat[p * rows : p * rows + EDGE, :] = head[p]
            flat[(p + 1) * rows - EDGE : (p + 1) * rows, :] = tail[p]
        for lane in range(0, depth, 128):
            lanes = slice(lane, lane + 128)
            for row in range(EDGE, rows - EDGE, 8):
                for p, item in enumerate(across(own, near, far, odd_x, row, lanes)):
                    flat[p * rows + row : p * rows + row + 8, lanes] = item
        crossed = z_pass(flat[...], 3).reshape(planes, rows, depth)
        outer[:, :EDGE] = crossed[:, :EDGE]
        outer[:, EDGE:] = crossed[:, rows - EDGE :]
        inside = rows - 2 * RADIUS
        for p in range(planes):
            tilted, slope = tilt(cone_rows(crossed[p], 0)[:inside])
            tilted_out[p] = tilted
            part = sens[p, RADIUS : rows - RADIUS] * slope
            chain[p] = part
            middle[p] = cone_rows(part, 0)[: rows - 2 * EDGE]
        keep[...], send[...] = halves(middle[...])

    def chain_kernel(outer, chain_in, near, far, sens, tilted_out, keep, send, halo, ys):
        planes, rows, depth = sens.shape
        low, high = ordered(is_odd("gy"), near[...], far[...])
        for p in range(planes):
            halo[2 * EDGE * p : 2 * EDGE * p + EDGE, :] = low[p, :EDGE]
            halo[2 * EDGE * p + EDGE : 2 * EDGE * (p + 1), :] = high[p, :EDGE]
        beyond = z_pass(halo[...], 3).reshape(planes, 2 * EDGE, depth)
        for p in range(planes):
            top = jnp.concatenate([beyond[p, :EDGE], outer[p, :EDGE]], axis=0)
            bottom = jnp.concatenate([outer[p, EDGE:], beyond[p, EDGE:]], axis=0)
            tops, slope_top = tilt(cone_rows(top, 0)[:EDGE])
            bottoms, slope_bottom = tilt(cone_rows(bottom, 0)[:EDGE])
            tilted_out[p, :RADIUS] = tops[RADIUS:]
            tilted_out[p, RADIUS:] = bottoms[:RADIUS]
            above = jnp.concatenate([low[p, EDGE:], sens[p, :RADIUS]], axis=0) * slope_top
            below = jnp.concatenate([sens[p, rows - RADIUS :], high[p, EDGE:]], axis=0) * slope_bottom
            top = jnp.concatenate([above, chain_in[p, :EDGE]], axis=0)
            bottom = jnp.concatenate([chain_in[p, rows - EDGE - 2 * RADIUS :], below], axis=0)
            ys[p, :EDGE] = cone_rows(top, 0)[:EDGE]
            ys[p, EDGE:] = cone_rows(bottom, 0)[:EDGE]
        keep[...], send[...] = halves(ys[...])

    def project_kernel(inside, edges, projected):
        tilted = jnp.concatenate([edges[:, :RADIUS], inside[...], edges[:, RADIUS:]], axis=1)
        projected[...] = (TANH_LOW + tilted) * (1.0 / SCALE_SUM)

    def sum_y_kernel(own, from_y, total):
        total[...] = own[...] + flip_rows(from_y[...])

    def sum_x_kernel(own, from_x, total):
        total[...] = own[...] + flip_planes(from_x[...])

    def cross_part_kernel(own, near, far, out):
        planes, rows, depth = own.shape
        place = lax.rem(lax.axis_index("gx"), hx)
        first, last = place == 0, place == hx - 1
        for row in range(0, rows, 8):
            items = across(own, near, far, is_odd("gx"), row, slice(0, depth), first, last)
            for p, item in enumerate(items):
                out[p, row : row + 8, :] = item

    def finish_kernel(inner, outer, from_inner, from_outer, gradient, flat):
        planes, rows, depth = gradient.shape
        upper = lax.axis_index("gy") >= hy

        def whole(inner, outer):
            lines = jnp.concatenate([outer[:, :EDGE], inner, outer[:, EDGE:]], axis=1)
            return lines.reshape(planes * rows, depth // 2)

        mine = whole(inner[...], outer[...])
        other = whole(flip_rows(from_inner[...]), flip_rows(from_outer[...]))
        flat[:, : depth // 2] = jnp.where(upper, other, mine)
        flat[:, depth // 2 :] = jnp.where(upper, mine, other)
        gradient[...] = (z_pass(flat[...], 2) * (0.25 * WEIGHT)).reshape(planes, rows, depth)

    near_x = [(i, i ^ 1) for i in range(nx)]
    near_y = [(j, j ^ 1) for j in range(ny)]
    far_x = [(i, (i + (1 if i % 2 else -1)) % nx) for i in range(nx)]
    far_y = [(j, (j + (1 if j % 2 else -1)) % ny) for j in range(ny)]
    fold_far_x = [(a, b) for a, b in far_x if a // hx == b // hx and abs(a - b) == 1]
    mirror_x = [(i, nx - 1 - i) for i in range(nx)]
    mirror_y = [(j, ny - 1 - j) for j in range(ny)]

    def symmetrized(keep, send):
        part = keep.shape
        (total,) = run(sum_y_kernel, [part], (keep, lax.ppermute(send, "gy", mirror_y)))
        (total,) = run(sum_x_kernel, [part], (total, lax.ppermute(total, "gx", mirror_x)))
        far = lax.ppermute(total, "gx", fold_far_x)
        near = lax.ppermute(total, "gx", near_x)
        (smooth,) = run(cross_part_kernel, [part], (total, near, far))
        return smooth, lax.ppermute(smooth, "gy", mirror_y)

    def local(density, sensitivity):
        block = density.shape
        planes, rows, depth = block
        part = (planes, rows // 2, depth // 2)
        flat = pltpu.VMEM((planes * rows, depth), F32)
        far = lax.ppermute(density, "gx", far_x)
        near = lax.ppermute(density, "gx", near_x)
        own, sens = run(hold_kernel, [block, block], (density, sensitivity))
        to_near, to_far = run(
            cross_edges_kernel, [(planes, EDGE + RADIUS, depth)] * 2, (own, near, far, sens)
        )
        from_far = lax.ppermute(to_far, "gy", far_y)
        from_near = lax.ppermute(to_near, "gy", near_y)
        outer, inside, chain, *inner = run(
            cross_body_kernel,
            [
                (planes, 2 * EDGE, depth),
                (planes, rows - 2 * RADIUS, depth),
                (planes, rows - 2 * RADIUS, depth),
                part,
                part,
            ],
            (own, near, far, to_near, to_far, sens),
            (flat, pltpu.VMEM((planes, rows - 2 * EDGE, depth), F32)),
        )
        edges, *outer = run(
            chain_kernel,
            [(planes, 2 * RADIUS, depth), part, part],
            (outer, chain, from_near, from_far, sens),
            (pltpu.VMEM((planes * 2 * EDGE, depth), F32), pltpu.VMEM((planes, 2 * EDGE, depth), F32)),
        )
        (projected,) = run(project_kernel, [block], (inside, edges))
        inner, from_inner = symmetrized(*inner)
        outer, from_outer = symmetrized(*outer)
        (gradient,) = run(finish_kernel, [block], (inner, outer, from_inner, from_outer), (flat,))
        return projected, gradient

    return jax.shard_map(
        local,
        mesh=mesh,
        in_specs=(P("gx", "gy", None), P("gx", "gy", None)),
        out_specs=(P("gx", "gy", None), P("gx", "gy", None)),
        check_vma=False,
    )
```

```python
import math

import jax
import jax.numpy as jnp
from jax import lax
from jax.experimental import pallas as pl
from jax.experimental.pallas import tpu as pltpu
from jax.sharding import PartitionSpec as P

RADIUS = 8
WIDTH = RADIUS + 1
EDGE = 2 * RADIUS
SHARPNESS = 8.0
THRESHOLD = 0.5
TANH_LOW = math.tanh(SHARPNESS * THRESHOLD)
SCALE_SUM = TANH_LOW + math.tanh(SHARPNESS * (1.0 - THRESHOLD))
WEIGHT = 1.0 / float(WIDTH**6)
F32 = jnp.float32


def run(body, outs, args, scratch=(), passed=None):
    vmem, far = pl.BlockSpec(memory_space=pltpu.VMEM), pl.BlockSpec(memory_space=pl.ANY)
    last = len(args) - 1
    return pl.pallas_call(
        body,
        out_shape=[jax.ShapeDtypeStruct(shape, F32) for shape in outs],
        in_specs=[far if passed and k == last else vmem for k in range(len(args))],
        out_specs=[vmem if passed is None else far] * len(outs),
        scratch_shapes=list(scratch),
        input_output_aliases={last: 0} if passed else {},
        compiler_params=pltpu.CompilerParams(vmem_limit_bytes=24 * 1024 * 1024),
    )(*args)


def box_list(items):
    pairs = [a + b for a, b in zip(items, items[1:])]
    fours = [a + b for a, b in zip(pairs, pairs[2:])]
    eights = [a + b for a, b in zip(fours, fours[4:])]
    return [a + b for a, b in zip(eights, items[8:])]


def cone_list(items):
    return box_list(box_list(items))


def ahead(field, step, axis):
    return pltpu.roll(field, field.shape[axis] - step, axis)


def box_rows(field, axis):
    pairs = field + ahead(field, 1, axis)
    fours = pairs + ahead(pairs, 2, axis)
    eights = fours + ahead(fours, 4, axis)
    return eights + ahead(field, 8, axis)


def cone_rows(field, axis):
    return box_rows(box_rows(field, axis), axis)


def reverse_eights(field, axis):
    size = field.shape[axis]
    row = lax.broadcasted_iota(jnp.int32, field.shape, axis)
    for bit in (1, 2, 4):
        field = jnp.where(
            (row & bit) == 0, pltpu.roll(field, size - bit, axis), pltpu.roll(field, bit, axis)
        )
    return field


def flip_planes(field):
    return jnp.stack([field[p] for p in reversed(range(field.shape[0]))])


def flip_rows(field):
    field = reverse_eights(field, 1)
    groups = [field[:, r : r + 8] for r in range(0, field.shape[1], 8)]
    return jnp.concatenate(groups[::-1], axis=1)


def z_pass(field, pieces):
    count = field.shape[-1]
    row = lax.broadcasted_iota(jnp.int32, (count, count), 0)
    col = lax.broadcasted_iota(jnp.int32, (count, count), 1)
    gap = jnp.abs(row - col)
    taps = jnp.maximum(WIDTH - jnp.minimum(gap, count - gap), 0).astype(F32).astype(jnp.bfloat16)
    total = None
    for _ in range(pieces):
        piece = field.astype(jnp.bfloat16)
        field = field - piece.astype(F32)
        part = jnp.dot(piece, taps, preferred_element_type=F32)
        total = part if total is None else total + part
    return total


def solution(mesh):
    nx, ny = mesh.shape["gx"], mesh.shape["gy"]
    hx, hy = nx // 2, ny // 2

    def ordered(odd, near, far):
        return jnp.where(odd, near, far), jnp.where(odd, far, near)

    def is_odd(axis):
        return lax.rem(lax.axis_index(axis), 2) == 1

    def across(own, near, far, odd, row, lanes, first=None, last=None):
        planes = own.shape[0]
        rows = slice(row, row + 8)
        mine = [own[p, rows, lanes] for p in range(planes)]
        before, after = [], []
        for p in range(planes):
            b, a = ordered(odd, near[p, rows, lanes], far[p, rows, lanes])
            before.append(b if first is None else jnp.where(first, mine[-1 - p], b))
            after.append(a if last is None else jnp.where(last, mine[-1 - p], a))
        return cone_list(before + mine + after)

    def tilt(total):
        tilted = jnp.tanh(SHARPNESS * (total * WEIGHT - THRESHOLD))
        return tilted, (1.0 - tilted * tilted) * (SHARPNESS / SCALE_SUM)

    def halves(field):
        half = field.shape[-1] // 2
        upper = lax.axis_index("gy") >= hy
        low, high = field[..., :half], field[..., half:]
        return jnp.where(upper, high, low), jnp.where(upper, low, high)

    def hold_kernel(first, second, first_out, second_out):
        first_out[...] = first[...]
        second_out[...] = second[...]

    def cross_edges_kernel(own, near, far, sens, to_near, to_far):
        planes, rows, depth = own.shape
        odd_x, odd_y = is_odd("gx"), is_odd("gy")
        for lane in range(0, depth, 128):
            lanes = slice(lane, lane + 128)
            for row in range(0, EDGE, 8):
                heads = across(own, near, far, odd_x, row, lanes)
                tails = across(own, near, far, odd_x, rows - EDGE + row, lanes)
                for p, (head, tail) in enumerate(zip(heads, tails)):
                    to_near[p, row : row + 8, lanes] = jnp.where(odd_y, head, tail)
                    to_far[p, row : row + 8, lanes] = jnp.where(odd_y, tail, head)
        head, tail = sens[:, :RADIUS], sens[:, rows - RADIUS :]
        to_near[:, EDGE:] = jnp.where(odd_y, head, tail)
        to_far[:, EDGE:] = jnp.where(odd_y, tail, head)

    def cross_body_kernel(own, near, far, edge_near, edge_far, sens, outer, tilted_out, chain, keep, send, flat, middle):
        planes, rows, depth = own.shape
        odd_x = is_odd("gx")
        head, tail = ordered(is_odd("gy"), edge_near[:, :EDGE], edge_far[:, :EDGE])
        for p in range(planes):
            flat[p * rows : p * rows + EDGE, :] = head[p]
            flat[(p + 1) * rows - EDGE : (p + 1) * rows, :] = tail[p]
        for lane in range(0, depth, 128):
            lanes = slice(lane, lane + 128)
            for row in range(EDGE, rows - EDGE, 8):
                for p, item in enumerate(across(own, near, far, odd_x, row, lanes)):
                    flat[p * rows + row : p * rows + row + 8, lanes] = item
        crossed = z_pass(flat[...], 3).reshape(planes, rows, depth)
        outer[:, :EDGE] = crossed[:, :EDGE]
        outer[:, EDGE:] = crossed[:, rows - EDGE :]
        inside = rows - 2 * RADIUS
        for p in range(planes):
            tilted, slope = tilt(cone_rows(crossed[p], 0)[:inside])
            tilted_out[p] = tilted
            part = sens[p, RADIUS : rows - RADIUS] * slope
            chain[p] = part
            middle[p] = cone_rows(part, 0)[: rows - 2 * EDGE]
        keep[...], send[...] = halves(middle[...])

    def chain_kernel(outer, chain_in, near, far, sens, tilted_out, keep, send, halo, ys):
        planes, rows, depth = sens.shape
        low, high = ordered(is_odd("gy"), near[...], far[...])
        for p in range(planes):
            halo[2 * EDGE * p : 2 * EDGE * p + EDGE, :] = low[p, :EDGE]
            halo[2 * EDGE * p + EDGE : 2 * EDGE * (p + 1), :] = high[p, :EDGE]
        beyond = z_pass(halo[...], 3).reshape(planes, 2 * EDGE, depth)
        for p in range(planes):
            top = jnp.concatenate([beyond[p, :EDGE], outer[p, :EDGE]], axis=0)
            bottom = jnp.concatenate([outer[p, EDGE:], beyond[p, EDGE:]], axis=0)
            tops, slope_top = tilt(cone_rows(top, 0)[:EDGE])
            bottoms, slope_bottom = tilt(cone_rows(bottom, 0)[:EDGE])
            tilted_out[p, :RADIUS] = tops[RADIUS:]
            tilted_out[p, RADIUS:] = bottoms[:RADIUS]
            above = jnp.concatenate([low[p, EDGE:], sens[p, :RADIUS]], axis=0) * slope_top
            below = jnp.concatenate([sens[p, rows - RADIUS :], high[p, EDGE:]], axis=0) * slope_bottom
            top = jnp.concatenate([above, chain_in[p, :EDGE]], axis=0)
            bottom = jnp.concatenate([chain_in[p, rows - EDGE - 2 * RADIUS :], below], axis=0)
            ys[p, :EDGE] = cone_rows(top, 0)[:EDGE]
            ys[p, EDGE:] = cone_rows(bottom, 0)[:EDGE]
        keep[...], send[...] = halves(ys[...])

    def project_kernel(inside, edges, projected):
        tilted = jnp.concatenate([edges[:, :RADIUS], inside[...], edges[:, RADIUS:]], axis=1)
        projected[...] = (TANH_LOW + tilted) * (1.0 / SCALE_SUM)

    def sum_y_kernel(own, from_y, total):
        total[...] = own[...] + flip_rows(from_y[...])

    def sum_x_kernel(own, from_x, total):
        total[...] = own[...] + flip_planes(from_x[...])

    def cross_part_kernel(own, near, far, out):
        planes, rows, depth = own.shape
        place = lax.rem(lax.axis_index("gx"), hx)
        first, last = place == 0, place == hx - 1
        for row in range(0, rows, 8):
            items = across(own, near, far, is_odd("gx"), row, slice(0, depth), first, last)
            for p, item in enumerate(items):
                out[p, row : row + 8, :] = item

    def smooth_z(own, from_y, held, flat):
        planes, rows, depth = held.shape
        upper = lax.axis_index("gy") >= hy
        mine = own[...].reshape(planes * rows, depth // 2)
        other = flip_rows(from_y[...]).reshape(planes * rows, depth // 2)
        flat[:, : depth // 2] = jnp.where(upper, other, mine)
        flat[:, depth // 2 :] = jnp.where(upper, mine, other)
        held[...] = (z_pass(flat[...], 2) * (0.25 * WEIGHT)).reshape(planes, rows, depth)

    def finish_inner_kernel(own, from_y, gradient, held, flat, sems):
        smooth_z(own, from_y, held, flat)
        inside = pl.ds(EDGE, held.shape[1])
        copy = pltpu.make_async_copy(held, gradient.at[:, inside], sems.at[0])
        copy.start()
        copy.wait()

    def finish_outer_kernel(own, from_y, _, gradient, held, flat, sems):
        smooth_z(own, from_y, held, flat)
        copies = [
            pltpu.make_async_copy(held.at[:, pl.ds(row, EDGE)], gradient.at[:, pl.ds(at, EDGE)], sems.at[k])
            for k, (row, at) in enumerate(((0, 0), (EDGE, gradient.shape[1] - EDGE)))
        ]
        for copy in copies:
            copy.start()
        for copy in copies:
            copy.wait()

    near_x = [(i, i ^ 1) for i in range(nx)]
    near_y = [(j, j ^ 1) for j in range(ny)]
    far_x = [(i, (i + (1 if i % 2 else -1)) % nx) for i in range(nx)]
    far_y = [(j, (j + (1 if j % 2 else -1)) % ny) for j in range(ny)]
    fold_far_x = [(a, b) for a, b in far_x if a // hx == b // hx and abs(a - b) == 1]
    mirror_x = [(i, nx - 1 - i) for i in range(nx)]
    mirror_y = [(j, ny - 1 - j) for j in range(ny)]

    def symmetrized(keep, send):
        part = keep.shape
        (total,) = run(sum_y_kernel, [part], (keep, lax.ppermute(send, "gy", mirror_y)))
        (total,) = run(sum_x_kernel, [part], (total, lax.ppermute(total, "gx", mirror_x)))
        far = lax.ppermute(total, "gx", fold_far_x)
        near = lax.ppermute(total, "gx", near_x)
        (smooth,) = run(cross_part_kernel, [part], (total, near, far))
        return smooth, lax.ppermute(smooth, "gy", mirror_y)

    def local(density, sensitivity):
        block = density.shape
        planes, rows, depth = block
        part = (planes, rows // 2, depth // 2)
        flat = pltpu.VMEM((planes * rows, depth), F32)
        far = lax.ppermute(density, "gx", far_x)
        near = lax.ppermute(density, "gx", near_x)
        own, sens = run(hold_kernel, [block, block], (density, sensitivity))
        to_near, to_far = run(
            cross_edges_kernel, [(planes, EDGE + RADIUS, depth)] * 2, (own, near, far, sens)
        )
        from_far = lax.ppermute(to_far, "gy", far_y)
        from_near = lax.ppermute(to_near, "gy", near_y)
        outer, inside, chain, *inner = run(
            cross_body_kernel,
            [
                (planes, 2 * EDGE, depth),
                (planes, rows - 2 * RADIUS, depth),
                (planes, rows - 2 * RADIUS, depth),
                part,
                part,
            ],
            (own, near, far, to_near, to_far, sens),
            (flat, pltpu.VMEM((planes, rows - 2 * EDGE, depth), F32)),
        )
        edges, *outer = run(
            chain_kernel,
            [(planes, 2 * RADIUS, depth), part, part],
            (outer, chain, from_near, from_far, sens),
            (pltpu.VMEM((planes * 2 * EDGE, depth), F32), pltpu.VMEM((planes, 2 * EDGE, depth), F32)),
        )
        (projected,) = run(project_kernel, [block], (inside, edges))
        inner, from_inner = symmetrized(*inner)
        outer, from_outer = symmetrized(*outer)
        scratch = (
            pltpu.VMEM((planes, rows // 2, depth), F32),
            pltpu.VMEM((planes * rows // 2, depth), F32),
            pltpu.SemaphoreType.DMA((2,)),
        )
        (gradient,) = run(finish_inner_kernel, [block], (inner, from_inner), scratch, 0)
        (gradient,) = run(finish_outer_kernel, [block], (outer, from_outer, gradient), scratch, 1)
        return projected, gradient

    return jax.shard_map(
        local,
        mesh=mesh,
        in_specs=(P("gx", "gy", None), P("gx", "gy", None)),
        out_specs=(P("gx", "gy", None), P("gx", "gy", None)),
        check_vma=False,
    )
```

```python
import math

import jax
import jax.numpy as jnp
from jax import lax
from jax.experimental import pallas as pl
from jax.experimental.pallas import tpu as pltpu
from jax.sharding import PartitionSpec as P

RADIUS = 8
WIDTH = RADIUS + 1
EDGE = 2 * RADIUS
SHARPNESS = 8.0
THRESHOLD = 0.5
TANH_LOW = math.tanh(SHARPNESS * THRESHOLD)
SCALE_SUM = TANH_LOW + math.tanh(SHARPNESS * (1.0 - THRESHOLD))
WEIGHT = 1.0 / float(WIDTH**6)
F32 = jnp.float32


def run(body, outs, args, scratch=(), passed=None):
    vmem, far = pl.BlockSpec(memory_space=pltpu.VMEM), pl.BlockSpec(memory_space=pl.ANY)
    last = len(args) - 1
    return pl.pallas_call(
        body,
        out_shape=[jax.ShapeDtypeStruct(shape, F32) for shape in outs],
        in_specs=[far if passed and k == last else vmem for k in range(len(args))],
        out_specs=[vmem if passed is None else far] * len(outs),
        scratch_shapes=list(scratch),
        input_output_aliases={last: 0} if passed else {},
        compiler_params=pltpu.CompilerParams(vmem_limit_bytes=24 * 1024 * 1024),
    )(*args)


def box_list(items):
    pairs = [a + b for a, b in zip(items, items[1:])]
    fours = [a + b for a, b in zip(pairs, pairs[2:])]
    eights = [a + b for a, b in zip(fours, fours[4:])]
    return [a + b for a, b in zip(eights, items[8:])]


def cone_list(items):
    return box_list(box_list(items))


def ahead(field, step, axis):
    return pltpu.roll(field, field.shape[axis] - step, axis)


def box_rows(field, axis):
    pairs = field + ahead(field, 1, axis)
    fours = pairs + ahead(pairs, 2, axis)
    eights = fours + ahead(fours, 4, axis)
    return eights + ahead(field, 8, axis)


def cone_rows(field, axis):
    return box_rows(box_rows(field, axis), axis)


def reverse_eights(field, axis):
    size = field.shape[axis]
    row = lax.broadcasted_iota(jnp.int32, field.shape, axis)
    for bit in (1, 2, 4):
        field = jnp.where(
            (row & bit) == 0, pltpu.roll(field, size - bit, axis), pltpu.roll(field, bit, axis)
        )
    return field


def flip_planes(field):
    return jnp.stack([field[p] for p in reversed(range(field.shape[0]))])


def flip_rows(field):
    field = reverse_eights(field, 1)
    groups = [field[:, r : r + 8] for r in range(0, field.shape[1], 8)]
    return jnp.concatenate(groups[::-1], axis=1)


def z_pass(field, pieces):
    count = field.shape[-1]
    row = lax.broadcasted_iota(jnp.int32, (count, count), 0)
    col = lax.broadcasted_iota(jnp.int32, (count, count), 1)
    gap = jnp.abs(row - col)
    taps = jnp.maximum(WIDTH - jnp.minimum(gap, count - gap), 0).astype(F32).astype(jnp.bfloat16)
    total = None
    for _ in range(pieces):
        piece = field.astype(jnp.bfloat16)
        field = field - piece.astype(F32)
        part = jnp.dot(piece, taps, preferred_element_type=F32)
        total = part if total is None else total + part
    return total


def solution(mesh):
    nx, ny = mesh.shape["gx"], mesh.shape["gy"]
    hx, hy = nx // 2, ny // 2

    def ordered(odd, near, far):
        return jnp.where(odd, near, far), jnp.where(odd, far, near)

    def is_odd(axis):
        return lax.rem(lax.axis_index(axis), 2) == 1

    def across(own, near, far, odd, row, lanes, first=None, last=None):
        planes = own.shape[0]
        rows = slice(row, row + 8)
        mine = [own[p, rows, lanes] for p in range(planes)]
        before, after = [], []
        for p in range(planes):
            b, a = ordered(odd, near[p, rows, lanes], far[p, rows, lanes])
            before.append(b if first is None else jnp.where(first, mine[-1 - p], b))
            after.append(a if last is None else jnp.where(last, mine[-1 - p], a))
        return cone_list(before + mine + after)

    def tilt(total):
        tilted = jnp.tanh(SHARPNESS * (total * WEIGHT - THRESHOLD))
        return tilted, (1.0 - tilted * tilted) * (SHARPNESS / SCALE_SUM)

    def halves(field):
        half = field.shape[-1] // 2
        upper = lax.axis_index("gy") >= hy
        low, high = field[..., :half], field[..., half:]
        return jnp.where(upper, high, low), jnp.where(upper, low, high)

    def hold_kernel(first, second, first_out, second_out):
        first_out[...] = first[...]
        second_out[...] = second[...]

    def cross_edges_kernel(own, near, far, sens, to_near, to_far):
        planes, rows, depth = own.shape
        odd_x, odd_y = is_odd("gx"), is_odd("gy")
        for lane in range(0, depth, 128):
            lanes = slice(lane, lane + 128)
            for row in range(0, EDGE, 8):
                heads = across(own, near, far, odd_x, row, lanes)
                tails = across(own, near, far, odd_x, rows - EDGE + row, lanes)
                for p, (head, tail) in enumerate(zip(heads, tails)):
                    to_near[p, row : row + 8, lanes] = jnp.where(odd_y, head, tail)
                    to_far[p, row : row + 8, lanes] = jnp.where(odd_y, tail, head)
        head, tail = sens[:, :RADIUS], sens[:, rows - RADIUS :]
        to_near[:, EDGE:] = jnp.where(odd_y, head, tail)
        to_far[:, EDGE:] = jnp.where(odd_y, tail, head)

    def cross_body_kernel(own, near, far, edge_near, edge_far, sens, outer, tilted_out, chain, keep, send, flat, middle):
        planes, rows, depth = own.shape
        odd_x = is_odd("gx")
        head, tail = ordered(is_odd("gy"), edge_near[:, :EDGE], edge_far[:, :EDGE])
        for p in range(planes):
            flat[p * rows : p * rows + EDGE, :] = head[p]
            flat[(p + 1) * rows - EDGE : (p + 1) * rows, :] = tail[p]
        for lane in range(0, depth, 128):
            lanes = slice(lane, lane + 128)
            for row in range(EDGE, rows - EDGE, 8):
                for p, item in enumerate(across(own, near, far, odd_x, row, lanes)):
                    flat[p * rows + row : p * rows + row + 8, lanes] = item
        crossed = z_pass(flat[...], 3).reshape(planes, rows, depth)
        outer[:, :EDGE] = crossed[:, :EDGE]
        outer[:, EDGE:] = crossed[:, rows - EDGE :]
        inside = rows - 2 * RADIUS
        for p in range(planes):
            tilted, slope = tilt(cone_rows(crossed[p], 0)[:inside])
            tilted_out[p] = tilted
            part = sens[p, RADIUS : rows - RADIUS] * slope
            chain[p] = part
            middle[p] = cone_rows(part, 0)[: rows - 2 * EDGE]
        keep[...], send[...] = halves(middle[...])

    def one_side(low, outer, chain, message, sens, put):
        planes, rows, depth = sens.shape
        halo = message[:, :EDGE].reshape(planes * EDGE, depth)
        beyond = z_pass(halo, 3).reshape(planes, EDGE, depth)

        def join(outside, inside):
            first, second = jnp.where(low, outside, inside), jnp.where(low, inside, outside)
            return jnp.concatenate([first, second], axis=0)

        for p in range(planes):
            inside = jnp.where(low, outer[p, :EDGE], outer[p, EDGE:])
            tilted, slope = tilt(cone_rows(join(beyond[p], inside), 0)[:EDGE])
            inside = jnp.where(low, sens[p, :RADIUS], sens[p, rows - RADIUS :])
            part = join(message[p, EDGE:], inside) * slope
            inside = jnp.where(low, chain[p, :EDGE], chain[p, rows - 2 * RADIUS - EDGE :])
            at_edge = jnp.where(low, tilted[RADIUS:], tilted[:RADIUS])
            put(p, at_edge, cone_rows(join(part, inside), 0)[:EDGE])

    def near_kernel(outer, chain, message, sens, tilted_out, ys):
        def put(p, tilted, part):
            tilted_out[p] = tilted
            ys[p] = part

        one_side(is_odd("gy"), outer, chain, message, sens, put)

    def chain_kernel(outer, chain, message, sens, near_tilted, near_ys, tilted_out, keep, send, ys):
        odd = is_odd("gy")

        def put(p, tilted, part):
            low, high = ordered(odd, near_tilted[p], tilted)
            tilted_out[p, :RADIUS] = low
            tilted_out[p, RADIUS:] = high
            low, high = ordered(odd, near_ys[p], part)
            ys[p, :EDGE] = low
            ys[p, EDGE:] = high

        one_side(jnp.logical_not(odd), outer, chain, message, sens, put)
        keep[...], send[...] = halves(ys[...])

    def project_kernel(inside, edges, projected):
        tilted = jnp.concatenate([edges[:, :RADIUS], inside[...], edges[:, RADIUS:]], axis=1)
        projected[...] = (TANH_LOW + tilted) * (1.0 / SCALE_SUM)

    def sum_y_kernel(own, from_y, total):
        total[...] = own[...] + flip_rows(from_y[...])

    def sum_x_kernel(own, from_x, total):
        total[...] = own[...] + flip_planes(from_x[...])

    def cross_part_kernel(own, near, far, out):
        planes, rows, depth = own.shape
        place = lax.rem(lax.axis_index("gx"), hx)
        first, last = place == 0, place == hx - 1
        for row in range(0, rows, 8):
            items = across(own, near, far, is_odd("gx"), row, slice(0, depth), first, last)
            for p, item in enumerate(items):
                out[p, row : row + 8, :] = item

    def smooth_z(own, from_y, held, flat):
        planes, rows, depth = held.shape
        upper = lax.axis_index("gy") >= hy
        mine = own[...].reshape(planes * rows, depth // 2)
        other = flip_rows(from_y[...]).reshape(planes * rows, depth // 2)
        flat[:, : depth // 2] = jnp.where(upper, other, mine)
        flat[:, depth // 2 :] = jnp.where(upper, mine, other)
        held[...] = (z_pass(flat[...], 2) * (0.25 * WEIGHT)).reshape(planes, rows, depth)

    def finish_inner_kernel(own, from_y, gradient, held, flat, sems):
        smooth_z(own, from_y, held, flat)
        inside = pl.ds(EDGE, held.shape[1])
        copy = pltpu.make_async_copy(held, gradient.at[:, inside], sems.at[0])
        copy.start()
        copy.wait()

    def finish_outer_kernel(own, from_y, _, gradient, held, flat, sems):
        smooth_z(own, from_y, held, flat)
        copies = [
            pltpu.make_async_copy(held.at[:, pl.ds(row, EDGE)], gradient.at[:, pl.ds(at, EDGE)], sems.at[k])
            for k, (row, at) in enumerate(((0, 0), (EDGE, gradient.shape[1] - EDGE)))
        ]
        for copy in copies:
            copy.start()
        for copy in copies:
            copy.wait()

    near_x = [(i, i ^ 1) for i in range(nx)]
    near_y = [(j, j ^ 1) for j in range(ny)]
    far_x = [(i, (i + (1 if i % 2 else -1)) % nx) for i in range(nx)]
    far_y = [(j, (j + (1 if j % 2 else -1)) % ny) for j in range(ny)]
    fold_far_x = [(a, b) for a, b in far_x if a // hx == b // hx and abs(a - b) == 1]
    mirror_x = [(i, nx - 1 - i) for i in range(nx)]
    mirror_y = [(j, ny - 1 - j) for j in range(ny)]

    def symmetrized(keep, send):
        part = keep.shape
        (total,) = run(sum_y_kernel, [part], (keep, lax.ppermute(send, "gy", mirror_y)))
        (total,) = run(sum_x_kernel, [part], (total, lax.ppermute(total, "gx", mirror_x)))
        far = lax.ppermute(total, "gx", fold_far_x)
        near = lax.ppermute(total, "gx", near_x)
        (smooth,) = run(cross_part_kernel, [part], (total, near, far))
        return smooth, lax.ppermute(smooth, "gy", mirror_y)

    def local(density, sensitivity):
        block = density.shape
        planes, rows, depth = block
        part = (planes, rows // 2, depth // 2)
        flat = pltpu.VMEM((planes * rows, depth), F32)
        far = lax.ppermute(density, "gx", far_x)
        near = lax.ppermute(density, "gx", near_x)
        own, sens = run(hold_kernel, [block, block], (density, sensitivity))
        to_near, to_far = run(
            cross_edges_kernel, [(planes, EDGE + RADIUS, depth)] * 2, (own, near, far, sens)
        )
        from_far = lax.ppermute(to_far, "gy", far_y)
        from_near = lax.ppermute(to_near, "gy", near_y)
        outer, inside, chain, *inner = run(
            cross_body_kernel,
            [
                (planes, 2 * EDGE, depth),
                (planes, rows - 2 * RADIUS, depth),
                (planes, rows - 2 * RADIUS, depth),
                part,
                part,
            ],
            (own, near, far, to_near, to_far, sens),
            (flat, pltpu.VMEM((planes, rows - 2 * EDGE, depth), F32)),
        )
        near_edge = run(
            near_kernel,
            [(planes, RADIUS, depth), (planes, EDGE, depth)],
            (outer, chain, from_near, sens),
        )
        edges, *outer = run(
            chain_kernel,
            [(planes, 2 * RADIUS, depth), part, part],
            (outer, chain, from_far, sens, *near_edge),
            (pltpu.VMEM((planes, 2 * EDGE, depth), F32),),
        )
        (projected,) = run(project_kernel, [block], (inside, edges))
        inner, from_inner = symmetrized(*inner)
        outer, from_outer = symmetrized(*outer)
        scratch = (
            pltpu.VMEM((planes, rows // 2, depth), F32),
            pltpu.VMEM((planes * rows // 2, depth), F32),
            pltpu.SemaphoreType.DMA((2,)),
        )
        (gradient,) = run(finish_inner_kernel, [block], (inner, from_inner), scratch, 0)
        (gradient,) = run(finish_outer_kernel, [block], (outer, from_outer, gradient), scratch, 1)
        return projected, gradient

    return jax.shard_map(
        local,
        mesh=mesh,
        in_specs=(P("gx", "gy", None), P("gx", "gy", None)),
        out_specs=(P("gx", "gy", None), P("gx", "gy", None)),
        check_vma=False,
    )
```
